32 devices in a mesh: ctx: 16 (over z, y, x), tp: 2 (over core).
Axes of the slice: x: 2, y: 2, z: 4, core: 2. Of those that a mesh axis runs over, the one named last changes fastest.
Arguments:
- tokens: bfloat16 [16384, 1536], P('ctx'), may hold values from -6 to 6
- w_query: bfloat16 [1536, 1536], P(None, 'tp'), may hold values from -0.15625 to 0.15625
- w_key: bfloat16 [1536, 1536], P(None, 'tp'), may hold values from -0.15625 to 0.15625
- w_value: bfloat16 [1536, 1536], P(None, 'tp'), may hold values from -0.15625 to 0.15625
- w_out: bfloat16 [1536, 1536], P('tp'), may hold values from -0.15625 to 0.15625
Outputs:
- mixed: bfloat16 [16384, 1536], P('ctx', 'tp')
The draws below stay inside these ranges and needn't reach their ends.
All inputs are finite; a program needn't handle non-finite values.
Results may differ from the reference program's by a relative error of at most 0.0071.
Values may be sent and summed in bfloat16 or wider, within the bound.
A program may use at most 128 MiB of HBM per device.

```python
import jax
import jax.numpy as jnp
from jax import lax

D = 1536
HEADS = 12
HDIM = 128
BLK = 512
LENGTH = 16384


def shard_levels(stream_key, extent, pieces, low, largest):
    gain = 1.0
    for dim, blocks in pieces:
        steps = jax.random.uniform(jax.random.fold_in(jax.random.fold_in(stream_key, 6), dim), (blocks,), jnp.float32, low / len(pieces), largest / len(pieces))
        gain = gain * jnp.repeat(jnp.exp(steps), extent[dim] // blocks).reshape((-1,) + (1,) * (len(extent) - 1 - dim))
    return gain


def scatter_about(rng, extent, scale, reach, split=(), kind=jnp.bfloat16):
    values = jax.random.normal(rng, extent, jnp.float32) * scale
    if len(split) > 0:
        values = shard_levels(rng, extent, split, -0.22, 0.18) * values
    return jnp.clip(values, min=-reach, max=reach).astype(kind)


def setup_inputs(seed: int = 0) -> dict:
    arg_keys = jax.random.split(jax.random.key(seed), 6)
    return {
        "tokens": scatter_about(arg_keys[0], (LENGTH, D), 1.0, 6.0, ((0, 16),)),
        "w_query": scatter_about(arg_keys[1], (D, HEADS * HDIM), D ** -0.5, 0.15625, ((1, 2),)),
        "w_key": scatter_about(arg_keys[2], (D, HEADS * HDIM), D ** -0.5, 0.15625, ((1, 2),)),
        "w_value": scatter_about(arg_keys[3], (D, HEADS * HDIM), D ** -0.5, 0.15625, ((1, 2),)),
        "w_out": scatter_about(arg_keys[4], (HEADS * HDIM, D), (HEADS * HDIM) ** -0.5, 0.15625, ((0, 2),)),
    }


def reference(tokens, w_query, w_key, w_value, w_out):
    count = LENGTH // BLK
    blocks = tokens.reshape(count, BLK, D)
    causal = jnp.tril(jnp.ones((BLK, BLK), dtype=bool))

    def step(state, block):
        query = jax.nn.silu(jnp.dot(block, w_query, preferred_element_type=jnp.float32)).astype(jnp.bfloat16)
        keys = jax.nn.silu(jnp.dot(block, w_key, preferred_element_type=jnp.float32)).astype(jnp.bfloat16)
        values = jnp.dot(block, w_value, preferred_element_type=jnp.float32).astype(jnp.bfloat16)
        query = query.reshape(BLK, HEADS, HDIM).astype(jnp.float32)
        keys = keys.reshape(BLK, HEADS, HDIM).astype(jnp.float32)
        values = values.reshape(BLK, HEADS, HDIM).astype(jnp.float32)
        block_state = jnp.einsum('shd,she->hde', keys, values)
        carried = state.astype(jnp.bfloat16).astype(jnp.float32)
        scores = jnp.einsum('shd,thd->hst', query, keys)
        scores = jnp.where(causal[None], scores, 0.0).astype(jnp.bfloat16).astype(jnp.float32)
        attended = jnp.einsum('hst,the->she', scores, values) + jnp.einsum('shd,hde->she', query, carried)
        meansq = lax.optimization_barrier(jnp.mean(attended * attended, axis=-1, keepdims=True))
        normed = (attended * lax.rsqrt(meansq + 1e-06)).astype(jnp.bfloat16).reshape(BLK, HEADS * HDIM)
        mixed = jnp.dot(normed, w_out, preferred_element_type=jnp.float32).astype(jnp.bfloat16)
        return (state + block_state, mixed)
    start = jnp.zeros((HEADS, HDIM, HDIM), jnp.float32)
    _, outputs = lax.scan(step, start, blocks)
    return outputs.reshape(LENGTH, D)
```

```python
import functools

import jax
import jax.numpy as jnp
from jax import lax
from jax.experimental import pallas as pl
from jax.experimental.pallas import tpu as pltpu
from jax.sharding import PartitionSpec as P

HDIM = 128
PAIR = 2 * HDIM
CHUNK = 256
TILE = 512
GROUP = 4
MESH = pl.DeviceIdType.MESH
F32 = jnp.float32
BF16 = jnp.bfloat16


def silu(u):
    return u * (0.5 * jnp.tanh(0.5 * u) + 0.5)


def dot(a, b):
    return jnp.dot(a, b, preferred_element_type=F32)


def kernel(
    n_ctx,
    tok_hbm,
    wq_hbm,
    wk_hbm,
    wv_hbm,
    wo_hbm,
    out_hbm,
    tok,
    wq,
    wk,
    wv,
    wo_own,
    wo_peer,
    q_v,
    k_v,
    v_v,
    att,
    within,
    run,
    normed,
    normed_peer,
    acc,
    out_v,
    p1_send,
    p1_recv,
    p2_send,
    p2_recv,
    p3_send,
    p3_recv,
    tok_sem,
    w_sem,
    wo_sem,
    out_sem,
    wo_ssem,
    wo_rsem,
    s1,
    r1,
    s2,
    r2,
    s3,
    r3,
    sn,
    rn,
):
    rows = tok.shape[0]
    tiles = rows // TILE
    per_tile = TILE // CHUNK
    cols = wq.shape[1]
    pairs = cols // PAIR
    out_cols = wo_own.shape[1]
    groups = n_ctx // GROUP
    me = lax.axis_index("ctx")
    t = lax.axis_index("tp")
    g = me // GROUP
    p = lax.rem(me, GROUP)
    peer = 1 - t

    barrier = pltpu.get_barrier_semaphore()
    for k in range(1, GROUP):
        pl.semaphore_signal(
            barrier,
            inc=1,
            device_id={"ctx": g * GROUP + lax.rem(p + k, GROUP)},
            device_id_type=MESH,
        )
    for k in range(1, groups):
        pl.semaphore_signal(
            barrier,
            inc=1,
            device_id={"ctx": lax.rem(g + k, groups) * GROUP + p},
            device_id_type=MESH,
        )
    pl.semaphore_signal(barrier, inc=1, device_id={"tp": peer}, device_id_type=MESH)

    def tok_copy(r):
        part = pl.ds(r * TILE, TILE)
        return pltpu.make_async_copy(tok_hbm.at[part], tok.at[part], tok_sem.at[r])

    def w_copy(which, i):
        part = pl.ds(i * PAIR, PAIR)
        src, dst = ((wk_hbm, wk), (wv_hbm, wv), (wq_hbm, wq))[which]
        return pltpu.make_async_copy(
            src.at[:, part], dst.at[:, part], w_sem.at[which, i]
        )

    def wo_cols(side):
        return pl.ds(pl.multiple_of(side * out_cols, 128), out_cols)

    wo_copy = pltpu.make_async_copy(wo_hbm.at[:, wo_cols(t)], wo_own, wo_sem)
    wo_remote = pltpu.make_async_remote_copy(
        src_ref=wo_hbm.at[:, wo_cols(peer)],
        dst_ref=wo_peer,
        send_sem=wo_ssem,
        recv_sem=wo_rsem,
        device_id={"tp": peer},
        device_id_type=MESH,
    )

    w_copy(0, 0).start()
    tok_copy(0).start()
    w_copy(1, 0).start()
    for r in range(1, tiles):
        tok_copy(r).start()
    for i in range(1, pairs):
        w_copy(0, i).start()
        w_copy(1, i).start()
    for i in range(pairs):
        w_copy(2, i).start()
    wo_copy.start()

    def p1_copy(i, k, slot, to):
        return pltpu.make_async_remote_copy(
            src_ref=p1_send.at[i, to],
            dst_ref=p1_recv.at[i, slot],
            send_sem=s1.at[i, k],
            recv_sem=r1.at[i, k],
            device_id={"ctx": g * GROUP + to},
            device_id_type=MESH,
        )

    def p2_copy(i, slot, to):
        return pltpu.make_async_remote_copy(
            src_ref=p2_send.at[i],
            dst_ref=p2_recv.at[i, slot],
            send_sem=s2.at[i, to],
            recv_sem=r2.at[i, slot],
            device_id={"ctx": to * GROUP + p},
            device_id_type=MESH,
        )

    def p3_copy(i, k, slot, to):
        return pltpu.make_async_remote_copy(
            src_ref=p3_send.at[i, to],
            dst_ref=p3_recv.at[i, slot],
            send_sem=s3.at[i, k],
            recv_sem=r3.at[i, k],
            device_id={"ctx": g * GROUP + to},
            device_id_type=MESH,
        )

    def after(k):
        return lax.rem(p + k, GROUP)

    def before(k):
        return lax.rem(p + GROUP - k, GROUP)

    def p1_start(i):
        p1_send[i] = run[...].astype(BF16).reshape(GROUP, PAIR // GROUP, HDIM)
        p1_recv[i, p] = p1_send[i, p]
        for k in range(1, GROUP):
            p1_copy(i, k, p, after(k)).start()

    def p1_finish(i):
        for k in range(1, GROUP):
            p1_copy(i, k, before(k), after(k)).wait_recv()
        total = p1_recv[i, 0].astype(F32)
        for j in range(1, GROUP):
            total = total + p1_recv[i, j].astype(F32)
        p2_send[i] = total.astype(BF16)
        for to in range(1, groups):

            @pl.when(to > g)
            def _():
                p2_copy(i, g, to).start()

    def p2_finish(i):
        base = run.at[pl.ds(0, PAIR // GROUP)]
        base[...] = jnp.zeros_like(base)
        for frm in range(groups - 1):

            @pl.when(frm < g)
            def _():
                p2_copy(i, frm, frm).wait_recv()
                base[...] += p2_recv[i, frm].astype(F32)

        prefix = base[...]
        for j in range(GROUP):
            p3_send[i, j] = prefix.astype(BF16)
            if j < GROUP - 1:
                prefix = prefix + p1_recv[i, j].astype(F32)
        p3_recv[i, p] = p3_send[i, p]
        for k in range(1, GROUP):
            p3_copy(i, k, p, after(k)).start()

    def p3_finish(i):
        for k in range(1, GROUP):
            p3_copy(i, k, before(k), after(k)).wait_recv()

    def tile_rows(r):
        return pl.ds(pl.multiple_of(r * TILE, TILE), TILE)

    def kv_stage(i):
        cs = slice(i * PAIR, (i + 1) * PAIR)
        w_copy(0, i).wait()
        for r in range(tiles):
            if i == 0:
                tok_copy(r).wait()
            rs = slice(r * TILE, (r + 1) * TILE)
            keys = silu(dot(tok[rs, :], wk[:, cs])).astype(BF16)
            k_v[rs, cs] = keys
            if r == 0:
                w_copy(1, i).wait()
            vals = dot(tok[rs, :], wv[:, cs]).astype(BF16)
            v_v[rs, cs] = vals
            for c in range(per_tile):
                at = slice(c * CHUNK, (c + 1) * CHUNK)
                both = lax.dot_general(
                    keys[at],
                    vals[at],
                    (((0,), (0,)), ((), ())),
                    preferred_element_type=F32,
                )
                state = jnp.concatenate([both[:HDIM, :HDIM], both[HDIM:, HDIM:]], axis=0)
                idx = r * per_tile + c
                if idx == 0:
                    within[i, 0] = jnp.zeros_like(state)
                    run[...] = state
                else:
                    sofar = run[...]
                    within[i, idx] = sofar
                    run[...] = sofar + state

    causal = lax.broadcasted_iota(jnp.int32, (CHUNK, CHUNK), 0) >= lax.broadcasted_iota(
        jnp.int32, (CHUNK, CHUNK), 1
    )

    def qa_stage(i):
        cs = slice(i * PAIR, (i + 1) * PAIR)
        w_copy(2, i).wait()
        for r in range(tiles):
            rs = slice(r * TILE, (r + 1) * TILE)
            query = silu(dot(tok[rs, :], wq[:, cs])).astype(BF16)
            q_v[rs, cs] = query
            for c in range(per_tile):
                at = slice(r * TILE + c * CHUNK, r * TILE + (c + 1) * CHUNK)
                for h in range(2):
                    hs = slice(i * PAIR + h * HDIM, i * PAIR + (h + 1) * HDIM)
                    s = lax.dot_general(
                        query[c * CHUNK : (c + 1) * CHUNK, h * HDIM : (h + 1) * HDIM],
                        k_v[at, hs],
                        (((1,), (1,)), ((), ())),
                        preferred_element_type=F32,
                    )
                    s = jnp.where(causal, s, 0.0).astype(BF16)
                    att[at, hs] = dot(s, v_v[at, hs])

    def n_copy(i, c):
        part = (pl.ds(c * CHUNK, CHUNK), pl.ds(i * PAIR, PAIR))
        return pltpu.make_async_remote_copy(
            src_ref=normed.at[part],
            dst_ref=normed_peer.at[part],
            send_sem=sn.at[i, c],
            recv_sem=rn.at[i, c],
            device_id={"tp": peer},
            device_id_type=MESH,
        )

    def c_stage(i):
        p3_finish(i)
        prefix = p3_recv[i].reshape(PAIR, HDIM).astype(F32)
        cs = slice(i * PAIR, (i + 1) * PAIR)
        zero = jnp.zeros((HDIM, HDIM), BF16)
        for c in range(rows // CHUNK):
            at = slice(c * CHUNK, (c + 1) * CHUNK)
            carried = (prefix + within[i, c]).astype(BF16)
            diag = jnp.concatenate(
                [
                    jnp.concatenate([carried[:HDIM], zero], axis=1),
                    jnp.concatenate([zero, carried[HDIM:]], axis=1),
                ],
                axis=0,
            )
            full = att[at, cs] + dot(q_v[at, cs], diag)
            for h in range(2):
                x = full[:, h * HDIM : (h + 1) * HDIM]
                meansq = jnp.mean(x * x, axis=-1, keepdims=True)
                hs = slice(i * PAIR + h * HDIM, i * PAIR + (h + 1) * HDIM)
                normed[at, hs] = (x * lax.rsqrt(meansq + 1e-06)).astype(BF16)
            n_copy(i, c).start()

    kv_stage(0)
    pl.semaphore_wait(barrier, GROUP - 1 + groups - 1 + 1)
    p1_start(0)
    wo_remote.start()
    kv_stage(1)
    p1_start(1)
    p1_finish(0)
    kv_stage(2)
    p1_start(2)
    p2_finish(0)
    p1_finish(1)
    qa_stage(0)
    p2_finish(1)
    p1_finish(2)
    qa_stage(1)
    p2_finish(2)
    qa_stage(2)
    for i in range(pairs):
        c_stage(i)

    wo_copy.wait()
    for r in range(tiles):
        rs = slice(r * TILE, (r + 1) * TILE)
        acc[rs, :] = dot(normed[rs, :], wo_own[...])
    wo_remote.wait_recv()

    def out_copy(c):
        part = pl.ds(c * CHUNK, CHUNK)
        return pltpu.make_async_copy(out_v.at[part], out_hbm.at[part], out_sem.at[c])

    for c in range(rows // CHUNK):
        at = slice(c * CHUNK, (c + 1) * CHUNK)
        for i in range(pairs):
            n_copy(i, c).wait_recv()
        out_v[at, :] = (acc[at, :] + dot(normed_peer[at, :], wo_peer[...])).astype(BF16)
        out_copy(c).start()

    wo_remote.wait_send()
    for i in range(pairs):
        for k in range(1, GROUP):
            p1_copy(i, k, p, after(k)).wait_send()
            p3_copy(i, k, p, after(k)).wait_send()
        for to in range(1, groups):

            @pl.when(to > g)
            def _():
                p2_copy(i, g, to).wait_send()

        for c in range(rows // CHUNK):
            n_copy(i, c).wait_send()
    for c in range(rows // CHUNK):
        out_copy(c).wait()


def body(n_ctx, tokens, w_query, w_key, w_value, w_out):
    rows, width = tokens.shape
    cols = w_query.shape[1]
    out_cols = w_out.shape[1] // 2
    pairs = cols // PAIR
    chunks = rows // CHUNK
    groups = n_ctx // GROUP
    quarter = PAIR // GROUP
    dma = pltpu.SemaphoreType.DMA
    vmem = pltpu.VMEM
    return pl.pallas_call(
        functools.partial(kernel, n_ctx),
        out_shape=jax.ShapeDtypeStruct((rows, out_cols), BF16),
        in_specs=[pl.BlockSpec(memory_space=pl.ANY)] * 5,
        out_specs=pl.BlockSpec(memory_space=pl.ANY),
        scratch_shapes=[
            vmem((rows, width), BF16),
            vmem((width, cols), BF16),
            vmem((width, cols), BF16),
            vmem((width, cols), BF16),
            vmem((cols, out_cols), BF16),
            vmem((cols, out_cols), BF16),
            vmem((rows, cols), BF16),
            vmem((rows, cols), BF16),
            vmem((rows, cols), BF16),
            vmem((rows, cols), F32),
            vmem((pairs, chunks, PAIR, HDIM), F32),
            vmem((PAIR, HDIM), F32),
            vmem((rows, cols), BF16),
            vmem((rows, cols), BF16),
            vmem((rows, out_cols), F32),
            vmem((rows, out_cols), BF16),
            vmem((pairs, GROUP, quarter, HDIM), BF16),
            vmem((pairs, GROUP, quarter, HDIM), BF16),
            vmem((pairs, quarter, HDIM), BF16),
            vmem((pairs, groups, quarter, HDIM), BF16),
            vmem((pairs, GROUP, quarter, HDIM), BF16),
            vmem((pairs, GROUP, quarter, HDIM), BF16),
            dma((rows // TILE,)),
            dma((3, pairs)),
            dma,
            dma((chunks,)),
            dma,
            dma,
            dma((pairs, GROUP)),
            dma((pairs, GROUP)),
            dma((pairs, groups)),
            dma((pairs, groups)),
            dma((pairs, GROUP)),
            dma((pairs, GROUP)),
            dma((pairs, chunks)),
            dma((pairs, chunks)),
        ],
        compiler_params=pltpu.CompilerParams(
            collective_id=0, has_side_effects=True, vmem_limit_bytes=56 * 1024 * 1024
        ),
        cost_estimate=pl.CostEstimate(
            flops=2 * rows * (3 * width * cols + 2 * cols * out_cols + 4 * CHUNK * cols),
            bytes_accessed=2 * (rows * width + 5 * width * cols),
            transcendentals=2 * rows * cols,
        ),
    )(tokens, w_query, w_key, w_value, w_out)


def solution(mesh):
    return jax.shard_map(
        functools.partial(body, mesh.shape["ctx"]),
        mesh=mesh,
        in_specs=(P("ctx", None), P(None, "tp"), P(None, "tp"), P(None, "tp"), P("tp", None)),
        out_specs=P("ctx", "tp"),
        check_vma=False,
    )
```

```python
import functools

import jax
import jax.numpy as jnp
from jax import lax
from jax.experimental import pallas as pl
from jax.experimental.pallas import tpu as pltpu
from jax.sharding import PartitionSpec as P

HDIM = 128
PAIR = 2 * HDIM
CHUNK = 256
TILE = 512
GROUP = 4
MESH = pl.DeviceIdType.MESH
F32 = jnp.float32
BF16 = jnp.bfloat16


def silu(u):
    return u * (0.5 * jnp.tanh(0.5 * u) + 0.5)


def dot(a, b):
    return jnp.dot(a, b, preferred_element_type=F32)


def kernel(
    n_ctx,
    tok_hbm,
    wq_hbm,
    wk_hbm,
    wv_hbm,
    wo_hbm,
    out_hbm,
    tok,
    wq,
    wk,
    wv,
    wo_own,
    wo_peer,
    q_v,
    k_v,
    v_v,
    att,
    within,
    run,
    normed,
    normed_peer,
    acc,
    out_v,
    p1_send,
    p1_recv,
    p2_send,
    p2_recv,
    p3_send,
    p3_recv,
    tok_sem,
    w_sem,
    wo_sem,
    out_sem,
    wo_ssem,
    wo_rsem,
    s1,
    r1,
    s2,
    r2,
    s3,
    r3,
    sn,
    rn,
):
    rows = tok.shape[0]
    tiles = rows // TILE
    per_tile = TILE // CHUNK
    cols = wq.shape[1]
    pairs = cols // PAIR
    out_cols = wo_own.shape[1]
    groups = n_ctx // GROUP
    me = lax.axis_index("ctx")
    t = lax.axis_index("tp")
    g = me // GROUP
    p = lax.rem(me, GROUP)
    peer = 1 - t

    barrier = pltpu.get_barrier_semaphore()
    for k in range(1, GROUP):
        pl.semaphore_signal(
            barrier,
            inc=1,
            device_id={"ctx": g * GROUP + lax.rem(p + k, GROUP)},
            device_id_type=MESH,
        )
    for k in range(1, groups):
        pl.semaphore_signal(
            barrier,
            inc=1,
            device_id={"ctx": lax.rem(g + k, groups) * GROUP + p},
            device_id_type=MESH,
        )
    pl.semaphore_signal(barrier, inc=1, device_id={"tp": peer}, device_id_type=MESH)

    def tok_copy(r):
        part = pl.ds(r * TILE, TILE)
        return pltpu.make_async_copy(tok_hbm.at[part], tok.at[part], tok_sem.at[r])

    def w_copy(which, i):
        part = pl.ds(i * PAIR, PAIR)
        src, dst = ((wk_hbm, wk), (wv_hbm, wv), (wq_hbm, wq))[which]
        return pltpu.make_async_copy(
            src.at[:, part], dst.at[:, part], w_sem.at[which, i]
        )

    def wo_cols(side):
        return pl.ds(pl.multiple_of(side * out_cols, 128), out_cols)

    wo_copy = pltpu.make_async_copy(wo_hbm.at[:, wo_cols(t)], wo_own, wo_sem)
    wo_remote = pltpu.make_async_remote_copy(
        src_ref=wo_hbm.at[:, wo_cols(peer)],
        dst_ref=wo_peer,
        send_sem=wo_ssem,
        recv_sem=wo_rsem,
        device_id={"tp": peer},
        device_id_type=MESH,
    )

    w_copy(0, 0).start()
    tok_copy(0).start()
    w_copy(1, 0).start()

    def p1_copy(i, k, slot, to):
        return pltpu.make_async_remote_copy(
            src_ref=p1_send.at[i, to],
            dst_ref=p1_recv.at[i, slot],
            send_sem=s1.at[i, k],
            recv_sem=r1.at[i, k],
            device_id={"ctx": g * GROUP + to},
            device_id_type=MESH,
        )

    def p2_copy(i, slot, to):
        return pltpu.make_async_remote_copy(
            src_ref=p2_send.at[i],
            dst_ref=p2_recv.at[i, slot],
            send_sem=s2.at[i, to],
            recv_sem=r2.at[i, slot],
            device_id={"ctx": to * GROUP + p},
            device_id_type=MESH,
        )

    def p3_copy(i, k, slot, to):
        return pltpu.make_async_remote_copy(
            src_ref=p3_send.at[i, to],
            dst_ref=p3_recv.at[i, slot],
            send_sem=s3.at[i, k],
            recv_sem=r3.at[i, k],
            device_id={"ctx": g * GROUP + to},
            device_id_type=MESH,
        )

    def after(k):
        return lax.rem(p + k, GROUP)

    def before(k):
        return lax.rem(p + GROUP - k, GROUP)

    def p1_start(i):
        p1_send[i] = run[...].astype(BF16).reshape(GROUP, PAIR // GROUP, HDIM)
        p1_recv[i, p] = p1_send[i, p]
        for k in range(1, GROUP):
            p1_copy(i, k, p, after(k)).start()

    def p1_finish(i):
        for k in range(1, GROUP):
            p1_copy(i, k, before(k), after(k)).wait_recv()
        total = p1_recv[i, 0].astype(F32)
        for j in range(1, GROUP):
            total = total + p1_recv[i, j].astype(F32)
        p2_send[i] = total.astype(BF16)
        for to in range(1, groups):

            @pl.when(to > g)
            def _():
                p2_copy(i, g, to).start()

    def p2_finish(i):
        base = run.at[pl.ds(0, PAIR // GROUP)]
        base[...] = jnp.zeros_like(base)
        for frm in range(groups - 1):

            @pl.when(frm < g)
            def _():
                p2_copy(i, frm, frm).wait_recv()
                base[...] += p2_recv[i, frm].astype(F32)

        prefix = base[...]
        for j in range(GROUP):
            p3_send[i, j] = prefix.astype(BF16)
            if j < GROUP - 1:
                prefix = prefix + p1_recv[i, j].astype(F32)
        p3_recv[i, p] = p3_send[i, p]
        for k in range(1, GROUP):
            p3_copy(i, k, p, after(k)).start()

    def p3_finish(i):
        for k in range(1, GROUP):
            p3_copy(i, k, before(k), after(k)).wait_recv()

    def tile_rows(r):
        return pl.ds(pl.multiple_of(r * TILE, TILE), TILE)

    def kv_stage(i):
        cs = slice(i * PAIR, (i + 1) * PAIR)
        w_copy(0, i).wait()
        for r in range(tiles):
            if i == 0:
                tok_copy(r).wait()
                if r == 0:
                    for later in range(1, tiles):
                        tok_copy(later).start()
                if r == tiles - 1:
                    w_copy(0, 1).start()
                    w_copy(1, 1).start()
            rs = slice(r * TILE, (r + 1) * TILE)
            keys = silu(dot(tok[rs, :], wk[:, cs])).astype(BF16)
            k_v[rs, cs] = keys
            if r == 0:
                w_copy(1, i).wait()
            vals = dot(tok[rs, :], wv[:, cs]).astype(BF16)
            v_v[rs, cs] = vals
            for c in range(per_tile):
                at = slice(c * CHUNK, (c + 1) * CHUNK)
                both = lax.dot_general(
                    keys[at],
                    vals[at],
                    (((0,), (0,)), ((), ())),
                    preferred_element_type=F32,
                )
                state = jnp.concatenate([both[:HDIM, :HDIM], both[HDIM:, HDIM:]], axis=0)
                idx = r * per_tile + c
                if idx == 0:
                    within[i, 0] = jnp.zeros_like(state)
                    run[...] = state
                else:
                    sofar = run[...]
                    within[i, idx] = sofar
                    run[...] = sofar + state

    causal = lax.broadcasted_iota(jnp.int32, (CHUNK, CHUNK), 0) >= lax.broadcasted_iota(
        jnp.int32, (CHUNK, CHUNK), 1
    )

    def q_stage(i):
        cs = slice(i * PAIR, (i + 1) * PAIR)
        w_copy(2, i).wait()
        for r in range(tiles):
            rs = slice(r * TILE, (r + 1) * TILE)
            q_v[rs, cs] = silu(dot(tok[rs, :], wq[:, cs])).astype(BF16)

    def attn_stage(c):
        at = slice(c * CHUNK, (c + 1) * CHUNK)
        heads = [slice(h * HDIM, (h + 1) * HDIM) for h in range(cols // HDIM)]
        scores = []
        for hs in heads:
            s = lax.dot_general(
                q_v[at, hs],
                k_v[at, hs],
                (((1,), (1,)), ((), ())),
                preferred_element_type=F32,
            )
            scores.append(jnp.where(causal, s, 0.0).astype(BF16))
        for hs, s in zip(heads, scores):
            att[at, hs] = dot(s, v_v[at, hs])

    def n_copy(i, c):
        part = (pl.ds(c * CHUNK, CHUNK), pl.ds(i * PAIR, PAIR))
        return pltpu.make_async_remote_copy(
            src_ref=normed.at[part],
            dst_ref=normed_peer.at[part],
            send_sem=sn.at[i, c],
            recv_sem=rn.at[i, c],
            device_id={"tp": peer},
            device_id_type=MESH,
        )

    def c_stage(i):
        p3_finish(i)
        prefix = p3_recv[i].reshape(PAIR, HDIM).astype(F32)
        cs = slice(i * PAIR, (i + 1) * PAIR)
        zero = jnp.zeros((HDIM, HDIM), BF16)
        for c in range(rows // CHUNK):
            at = slice(c * CHUNK, (c + 1) * CHUNK)
            carried = (prefix + within[i, c]).astype(BF16)
            diag = jnp.concatenate(
                [
                    jnp.concatenate([carried[:HDIM], zero], axis=1),
                    jnp.concatenate([zero, carried[HDIM:]], axis=1),
                ],
                axis=0,
            )
            full = att[at, cs] + dot(q_v[at, cs], diag)
            for h in range(2):
                x = full[:, h * HDIM : (h + 1) * HDIM]
                meansq = jnp.mean(x * x, axis=-1, keepdims=True)
                hs = slice(i * PAIR + h * HDIM, i * PAIR + (h + 1) * HDIM)
                normed[at, hs] = (x * lax.rsqrt(meansq + 1e-06)).astype(BF16)
            n_copy(i, c).start()

    kv_stage(0)
    for i in range(2, pairs):
        w_copy(0, i).start()
        w_copy(1, i).start()
    pl.semaphore_wait(barrier, GROUP - 1 + groups - 1 + 1)
    p1_start(0)
    kv_stage(1)
    for i in range(pairs):
        w_copy(2, i).start()
    p1_start(1)
    p1_finish(0)
    wo_remote.start()
    wo_copy.start()
    kv_stage(2)
    p1_start(2)
    p2_finish(0)
    p1_finish(1)
    q_stage(0)
    q_stage(1)
    p2_finish(1)
    p1_finish(2)
    q_stage(2)
    attn_stage(0)
    attn_stage(1)
    p2_finish(2)
    for c in range(2, rows // CHUNK):
        attn_stage(c)
    c_stage(0)
    c_stage(1)
    wo_copy.wait()
    early = (pairs - 1) * PAIR
    for r in range(tiles):
        rs = slice(r * TILE, (r + 1) * TILE)
        acc[rs, :] = dot(normed[rs, :early], wo_own[:early, :])
    c_stage(2)
    for r in range(tiles):
        rs = slice(r * TILE, (r + 1) * TILE)
        acc[rs, :] += dot(normed[rs, early:], wo_own[early:, :])
    wo_remote.wait_recv()

    def out_copy(c):
        part = pl.ds(c * CHUNK, CHUNK)
        return pltpu.make_async_copy(out_v.at[part], out_hbm.at[part], out_sem.at[c])

    for c in range(rows // CHUNK):
        at = slice(c * CHUNK, (c + 1) * CHUNK)
        for i in range(pairs):
            n_copy(i, c).wait_recv()
        out_v[at, :] = (acc[at, :] + dot(normed_peer[at, :], wo_peer[...])).astype(BF16)
        out_copy(c).start()

    wo_remote.wait_send()
    for i in range(pairs):
        for k in range(1, GROUP):
            p1_copy(i, k, p, after(k)).wait_send()
            p3_copy(i, k, p, after(k)).wait_send()
        for to in range(1, groups):

            @pl.when(to > g)
            def _():
                p2_copy(i, g, to).wait_send()

        for c in range(rows // CHUNK):
            n_copy(i, c).wait_send()
    for c in range(rows // CHUNK):
        out_copy(c).wait()


def body(n_ctx, tokens, w_query, w_key, w_value, w_out):
    rows, width = tokens.shape
    cols = w_query.shape[1]
    out_cols = w_out.shape[1] // 2
    pairs = cols // PAIR
    chunks = rows // CHUNK
    groups = n_ctx // GROUP
    quarter = PAIR // GROUP
    dma = pltpu.SemaphoreType.DMA
    vmem = pltpu.VMEM
    return pl.pallas_call(
        functools.partial(kernel, n_ctx),
        out_shape=jax.ShapeDtypeStruct((rows, out_cols), BF16),
        in_specs=[pl.BlockSpec(memory_space=pl.ANY)] * 5,
        out_specs=pl.BlockSpec(memory_space=pl.ANY),
        scratch_shapes=[
            vmem((rows, width), BF16),
            vmem((width, cols), BF16),
            vmem((width, cols), BF16),
            vmem((width, cols), BF16),
            vmem((cols, out_cols), BF16),
            vmem((cols, out_cols), BF16),
            vmem((rows, cols), BF16),
            vmem((rows, cols), BF16),
            vmem((rows, cols), BF16),
            vmem((rows, cols), F32),
            vmem((pairs, chunks, PAIR, HDIM), F32),
            vmem((PAIR, HDIM), F32),
            vmem((rows, cols), BF16),
            vmem((rows, cols), BF16),
            vmem((rows, out_cols), F32),
            vmem((rows, out_cols), BF16),
            vmem((pairs, GROUP, quarter, HDIM), BF16),
            vmem((pairs, GROUP, quarter, HDIM), BF16),
            vmem((pairs, quarter, HDIM), BF16),
            vmem((pairs, groups, quarter, HDIM), BF16),
            vmem((pairs, GROUP, quarter, HDIM), BF16),
            vmem((pairs, GROUP, quarter, HDIM), BF16),
            dma((rows // TILE,)),
            dma((3, pairs)),
            dma,
            dma((chunks,)),
            dma,
            dma,
            dma((pairs, GROUP)),
            dma((pairs, GROUP)),
            dma((pairs, groups)),
            dma((pairs, groups)),
            dma((pairs, GROUP)),
            dma((pairs, GROUP)),
            dma((pairs, chunks)),
            dma((pairs, chunks)),
        ],
        compiler_params=pltpu.CompilerParams(
            collective_id=0, has_side_effects=True, vmem_limit_bytes=56 * 1024 * 1024
        ),
        cost_estimate=pl.CostEstimate(
            flops=2 * rows * (3 * width * cols + 2 * cols * out_cols + 4 * CHUNK * cols),
            bytes_accessed=2 * (rows * width + 5 * width * cols),
            transcendentals=2 * rows * cols,
        ),
    )(tokens, w_query, w_key, w_value, w_out)


def solution(mesh):
    return jax.shard_map(
        functools.partial(body, mesh.shape["ctx"]),
        mesh=mesh,
        in_specs=(P("ctx", None), P(None, "tp"), P(None, "tp"), P(None, "tp"), P("tp", None)),
        out_specs=P("ctx", "tp"),
        check_vma=False,
    )
```

```python
import functools

import jax
import jax.numpy as jnp
from jax import lax
from jax.experimental import pallas as pl
from jax.experimental.pallas import tpu as pltpu
from jax.sharding import PartitionSpec as P

HDIM = 128
PAIR = 2 * HDIM
CHUNK = 256
TILE = 512
GROUP = 4
MESH = pl.DeviceIdType.MESH
F32 = jnp.float32
BF16 = jnp.bfloat16


def silu(u):
    return u * (0.5 * jnp.tanh(0.5 * u) + 0.5)


def dot(a, b):
    return jnp.dot(a, b, preferred_element_type=F32)


def kernel(
    n_ctx,
    tok_hbm,
    wq_hbm,
    wk_hbm,
    wv_hbm,
    wo_hbm,
    out,
    tok,
    wq,
    wk,
    wv,
    wo_own,
    wo_peer,
    q_v,
    k_v,
    v_v,
    att,
    within,
    run,
    normed,
    normed_peer,
    acc,
    p1_send,
    p1_recv,
    p2_send,
    p2_recv,
    p3_send,
    p3_recv,
    tok_sem,
    w_sem,
    wo_sem,
    wo_ssem,
    wo_rsem,
    s1,
    r1,
    s2,
    r2,
    s3,
    r3,
    sn,
    rn,
):
    rows = tok.shape[0]
    tiles = rows // TILE
    per_tile = TILE // CHUNK
    cols = wq.shape[1]
    pairs = cols // PAIR
    out_cols = wo_own.shape[1]
    groups = n_ctx // GROUP
    me = lax.axis_index("ctx")
    t = lax.axis_index("tp")
    g = me // GROUP
    p = lax.rem(me, GROUP)
    peer = 1 - t

    barrier = pltpu.get_barrier_semaphore()
    for k in range(1, GROUP):
        pl.semaphore_signal(
            barrier,
            inc=1,
            device_id={"ctx": g * GROUP + lax.rem(p + k, GROUP)},
            device_id_type=MESH,
        )
    for k in range(1, groups):
        pl.semaphore_signal(
            barrier,
            inc=1,
            device_id={"ctx": lax.rem(g + k, groups) * GROUP + p},
            device_id_type=MESH,
        )
    pl.semaphore_signal(barrier, inc=1, device_id={"tp": peer}, device_id_type=MESH)

    def tok_copy(r):
        part = pl.ds(r * TILE, TILE)
        return pltpu.make_async_copy(tok_hbm.at[part], tok.at[part], tok_sem.at[r])

    def w_copy(which, i):
        part = pl.ds(i * PAIR, PAIR)
        src, dst = ((wk_hbm, wk), (wv_hbm, wv), (wq_hbm, wq))[which]
        return pltpu.make_async_copy(
            src.at[:, part], dst.at[:, part], w_sem.at[which, i]
        )

    def wo_cols(side):
        return pl.ds(pl.multiple_of(side * out_cols, 128), out_cols)

    wo_copy = pltpu.make_async_copy(wo_hbm.at[:, wo_cols(t)], wo_own, wo_sem)
    wo_remote = pltpu.make_async_remote_copy(
        src_ref=wo_hbm.at[:, wo_cols(peer)],
        dst_ref=wo_peer,
        send_sem=wo_ssem,
        recv_sem=wo_rsem,
        device_id={"tp": peer},
        device_id_type=MESH,
    )

    w_copy(0, 0).start()
    tok_copy(0).start()
    w_copy(1, 0).start()

    def p1_copy(i, k, slot, to):
        return pltpu.make_async_remote_copy(
            src_ref=p1_send.at[i, to],
            dst_ref=p1_recv.at[i, slot],
            send_sem=s1.at[i, k],
            recv_sem=r1.at[i, k],
            device_id={"ctx": g * GROUP + to},
            device_id_type=MESH,
        )

    def p2_copy(i, slot, to):
        return pltpu.make_async_remote_copy(
            src_ref=p2_send.at[i],
            dst_ref=p2_recv.at[i, slot],
            send_sem=s2.at[i, to],
            recv_sem=r2.at[i, slot],
            device_id={"ctx": to * GROUP + p},
            device_id_type=MESH,
        )

    def p3_copy(i, k, slot, to):
        return pltpu.make_async_remote_copy(
            src_ref=p3_send.at[i, to],
            dst_ref=p3_recv.at[i, slot],
            send_sem=s3.at[i, k],
            recv_sem=r3.at[i, k],
            device_id={"ctx": g * GROUP + to},
            device_id_type=MESH,
        )

    def after(k):
        return lax.rem(p + k, GROUP)

    def before(k):
        return lax.rem(p + GROUP - k, GROUP)

    def p1_start(i):
        p1_send[i] = run[...].astype(BF16).reshape(GROUP, PAIR // GROUP, HDIM)
        p1_recv[i, p] = p1_send[i, p]
        for k in range(1, GROUP):
            p1_copy(i, k, p, after(k)).start()

    def p1_finish(i):
        for k in range(1, GROUP):
            p1_copy(i, k, before(k), after(k)).wait_recv()
        total = p1_recv[i, 0].astype(F32)
        for j in range(1, GROUP):
            total = total + p1_recv[i, j].astype(F32)
        p2_send[i] = total.astype(BF16)
        for to in range(1, groups):

            @pl.when(to > g)
            def _():
                p2_copy(i, g, to).start()

    def p2_finish(i):
        base = run.at[pl.ds(0, PAIR // GROUP)]
        base[...] = jnp.zeros_like(base)
        for frm in range(groups - 1):

            @pl.when(frm < g)
            def _():
                p2_copy(i, frm, frm).wait_recv()
                base[...] += p2_recv[i, frm].astype(F32)

        prefix = base[...]
        for j in range(GROUP):
            p3_send[i, j] = prefix.astype(BF16)
            if j < GROUP - 1:
                prefix = prefix + p1_recv[i, j].astype(F32)
        p3_recv[i, p] = p3_send[i, p]
        for k in range(1, GROUP):
            p3_copy(i, k, p, after(k)).start()

    def p3_finish(i):
        for k in range(1, GROUP):
            p3_copy(i, k, before(k), after(k)).wait_recv()

    def tile_rows(r):
        return pl.ds(pl.multiple_of(r * TILE, TILE), TILE)

    def kv_stage(i):
        cs = slice(i * PAIR, (i + 1) * PAIR)
        w_copy(0, i).wait()
        for r in range(tiles):
            if i == 0:
                tok_copy(r).wait()
                if r == 0:
                    for later in range(1, tiles):
                        tok_copy(later).start()
                if r == tiles - 1:
                    w_copy(0, 1).start()
                    w_copy(1, 1).start()
            rs = slice(r * TILE, (r + 1) * TILE)
            keys = silu(dot(tok[rs, :], wk[:, cs])).astype(BF16)
            k_v[rs, cs] = keys
            if r == 0:
                w_copy(1, i).wait()
            vals = dot(tok[rs, :], wv[:, cs]).astype(BF16)
            v_v[rs, cs] = vals
            for c in range(per_tile):
                at = slice(c * CHUNK, (c + 1) * CHUNK)
                both = lax.dot_general(
                    keys[at],
                    vals[at],
                    (((0,), (0,)), ((), ())),
                    preferred_element_type=F32,
                )
                state = jnp.concatenate([both[:HDIM, :HDIM], both[HDIM:, HDIM:]], axis=0)
                idx = r * per_tile + c
                if idx == 0:
                    within[i, 0] = jnp.zeros_like(state)
                    run[...] = state
                else:
                    sofar = run[...]
                    within[i, idx] = sofar
                    run[...] = sofar + state

    causal = lax.broadcasted_iota(jnp.int32, (CHUNK, CHUNK), 0) >= lax.broadcasted_iota(
        jnp.int32, (CHUNK, CHUNK), 1
    )

    def q_stage(i):
        cs = slice(i * PAIR, (i + 1) * PAIR)
        w_copy(2, i).wait()
        for r in range(tiles):
            rs = slice(r * TILE, (r + 1) * TILE)
            q_v[rs, cs] = silu(dot(tok[rs, :], wq[:, cs])).astype(BF16)

    def attn_stage(c):
        at = slice(c * CHUNK, (c + 1) * CHUNK)
        heads = [slice(h * HDIM, (h + 1) * HDIM) for h in range(cols // HDIM)]
        scores = []
        for hs in heads:
            s = lax.dot_general(
                q_v[at, hs],
                k_v[at, hs],
                (((1,), (1,)), ((), ())),
                preferred_element_type=F32,
            )
            scores.append(jnp.where(causal, s, 0.0).astype(BF16))
        for hs, s in zip(heads, scores):
            att[at, hs] = dot(s, v_v[at, hs])

    def n_copy(i, c):
        part = (pl.ds(c * CHUNK, CHUNK), pl.ds(i * PAIR, PAIR))
        return pltpu.make_async_remote_copy(
            src_ref=normed.at[part],
            dst_ref=normed_peer.at[part],
            send_sem=sn.at[i, c],
            recv_sem=rn.at[i, c],
            device_id={"tp": peer},
            device_id_type=MESH,
        )

    def c_stage(i):
        p3_finish(i)
        prefix = p3_recv[i].reshape(PAIR, HDIM).astype(F32)
        cs = slice(i * PAIR, (i + 1) * PAIR)
        zero = jnp.zeros((HDIM, HDIM), BF16)
        for c in range(rows // CHUNK):
            at = slice(c * CHUNK, (c + 1) * CHUNK)
            carried = (prefix + within[i, c]).astype(BF16)
            diag = jnp.concatenate(
                [
                    jnp.concatenate([carried[:HDIM], zero], axis=1),
                    jnp.concatenate([zero, carried[HDIM:]], axis=1),
                ],
                axis=0,
            )
            full = att[at, cs] + dot(q_v[at, cs], diag)
            for h in range(2):
                x = full[:, h * HDIM : (h + 1) * HDIM]
                meansq = jnp.mean(x * x, axis=-1, keepdims=True)
                hs = slice(i * PAIR + h * HDIM, i * PAIR + (h + 1) * HDIM)
                normed[at, hs] = (x * lax.rsqrt(meansq + 1e-06)).astype(BF16)
            n_copy(i, c).start()

    kv_stage(0)
    for i in range(2, pairs):
        w_copy(0, i).start()
        w_copy(1, i).start()
    pl.semaphore_wait(barrier, GROUP - 1 + groups - 1 + 1)
    p1_start(0)
    kv_stage(1)
    for i in range(pairs):
        w_copy(2, i).start()
    p1_start(1)
    p1_finish(0)
    wo_remote.start()
    wo_copy.start()
    kv_stage(2)
    p1_start(2)
    p2_finish(0)
    p1_finish(1)
    q_stage(0)
    q_stage(1)
    q_stage(2)
    p2_finish(1)
    p1_finish(2)
    attn_stage(0)
    attn_stage(1)
    attn_stage(2)
    p2_finish(2)
    for c in range(3, rows // CHUNK):
        attn_stage(c)
    c_stage(0)
    c_stage(1)
    wo_copy.wait()
    wo_remote.wait_recv()
    early = (pairs - 1) * PAIR
    for r in range(tiles):
        rs = slice(r * TILE, (r + 1) * TILE)
        acc[rs, :] = dot(normed[rs, :early], wo_own[:early, :])
    for r in range(tiles):
        rs = slice(r * TILE, (r + 1) * TILE)
        for c in range(r * per_tile, (r + 1) * per_tile):
            for i in range(pairs - 1):
                n_copy(i, c).wait_recv()
        acc[rs, :] += dot(normed_peer[rs, :early], wo_peer[:early, :])
    c_stage(2)
    for r in range(tiles):
        rs = slice(r * TILE, (r + 1) * TILE)
        acc[rs, :] += dot(normed[rs, early:], wo_own[early:, :])

    for c in range(rows // CHUNK):
        at = slice(c * CHUNK, (c + 1) * CHUNK)
        n_copy(pairs - 1, c).wait_recv()
        out[at, :] = (acc[at, :] + dot(normed_peer[at, early:], wo_peer[early:, :])).astype(BF16)

    wo_remote.wait_send()
    for i in range(pairs):
        for k in range(1, GROUP):
            p1_copy(i, k, p, after(k)).wait_send()
            p3_copy(i, k, p, after(k)).wait_send()
        for to in range(1, groups):

            @pl.when(to > g)
            def _():
                p2_copy(i, g, to).wait_send()

        for c in range(rows // CHUNK):
            n_copy(i, c).wait_send()


def body(n_ctx, tokens, w_query, w_key, w_value, w_out):
    rows, width = tokens.shape
    cols = w_query.shape[1]
    out_cols = w_out.shape[1] // 2
    pairs = cols // PAIR
    chunks = rows // CHUNK
    groups = n_ctx // GROUP
    quarter = PAIR // GROUP
    dma = pltpu.SemaphoreType.DMA
    vmem = pltpu.VMEM
    return pl.pallas_call(
        functools.partial(kernel, n_ctx),
        out_shape=pltpu.VMEM((rows, out_cols), BF16),
        in_specs=[pl.BlockSpec(memory_space=pl.ANY)] * 5,
        out_specs=pl.BlockSpec(memory_space=pltpu.VMEM),
        scratch_shapes=[
            vmem((rows, width), BF16),
            vmem((width, cols), BF16),
            vmem((width, cols), BF16),
            vmem((width, cols), BF16),
            vmem((cols, out_cols), BF16),
            vmem((cols, out_cols), BF16),
            vmem((rows, cols), BF16),
            vmem((rows, cols), BF16),
            vmem((rows, cols), BF16),
            vmem((rows, cols), F32),
            vmem((pairs, chunks, PAIR, HDIM), F32),
            vmem((PAIR, HDIM), F32),
            vmem((rows, cols), BF16),
            vmem((rows, cols), BF16),
            vmem((rows, out_cols), F32),
            vmem((pairs, GROUP, quarter, HDIM), BF16),
            vmem((pairs, GROUP, quarter, HDIM), BF16),
            vmem((pairs, quarter, HDIM), BF16),
            vmem((pairs, groups, quarter, HDIM), BF16),
            vmem((pairs, GROUP, quarter, HDIM), BF16),
            vmem((pairs, GROUP, quarter, HDIM), BF16),
            dma((rows // TILE,)),
            dma((3, pairs)),
            dma,
            dma,
            dma,
            dma((pairs, GROUP)),
            dma((pairs, GROUP)),
            dma((pairs, groups)),
            dma((pairs, groups)),
            dma((pairs, GROUP)),
            dma((pairs, GROUP)),
            dma((pairs, chunks)),
            dma((pairs, chunks)),
        ],
        compiler_params=pltpu.CompilerParams(
            collective_id=0, has_side_effects=True, vmem_limit_bytes=56 * 1024 * 1024
        ),
        cost_estimate=pl.CostEstimate(
            flops=2 * rows * (3 * width * cols + 2 * cols * out_cols + 4 * CHUNK * cols),
            bytes_accessed=2 * (rows * width + 5 * width * cols),
            transcendentals=2 * rows * cols,
        ),
    )(tokens, w_query, w_key, w_value, w_out)


def solution(mesh):
    return jax.shard_map(
        functools.partial(body, mesh.shape["ctx"]),
        mesh=mesh,
        in_specs=(P("ctx", None), P(None, "tp"), P(None, "tp"), P(None, "tp"), P("tp", None)),
        out_specs=P("ctx", "tp"),
        check_vma=False,
    )
```
